256 devices in a mesh: replica: 8 (over y, z_hi), shard: 32 (over x, z_lo, core).
Axes of the slice: x: 4, y: 4, z: 8 (z_hi: 2, z_lo: 4; z = z_hi * 4 + z_lo), core: 2. Of those that a mesh axis runs over, the one named last changes fastest.
Arguments:
- hidden: bfloat16 [8, 4096, 11008], P('replica', 'shard'), may hold values from -6 to 6
- out_grad: bfloat16 [8, 4096, 2048], P('replica', 'shard'), may hold values from -6 to 6
- weights: float32 [8, 11008, 2048], P('replica', 'shard'), may hold values from -6 to 6
- round_index: int32 [1], replicated, may hold values from 0 to 7
Outputs:
- averaged: float32 [8, 11008, 2048], P('replica', 'shard')
- hidden_grad: bfloat16 [8, 4096, 11008], P('replica', 'shard')
The draws below stay inside these ranges and needn't reach their ends.
All inputs are finite; a program needn't handle non-finite values.
Results may differ from the reference program's by a relative error of at most 0.006.
Values may be sent and summed in bfloat16 or wider, within the bound.
No kernel may reach another device: no remote copies, remote signals or barrier semaphores. Data moves between devices by JAX's collectives and lax.ppermute only.
A program may use at most 128 MiB of HBM per device.

```python
import jax
import jax.numpy as jnp
from jax import lax

D = 2048
FF = 11008
TOKENS = 4096
REPLICAS = 8
N_REPLICA = 8


def level_of(own_key, extent, cuts, least, top_value):
    gain = 1.0
    for axis_at, shards_of in cuts:
        draws = jax.random.uniform(jax.random.fold_in(jax.random.fold_in(own_key, 6), axis_at), (shards_of,), jnp.float32, least / len(cuts), top_value / len(cuts))
        gain = gain * jnp.repeat(jnp.exp(draws), extent[axis_at] // shards_of).reshape((-1,) + (1,) * (len(extent) - 1 - axis_at))
    return gain


def bell_draw(stream_key, dims, deviation, reach, shards=(), held_as=jnp.bfloat16):
    gain = level_of(stream_key, dims, shards, -0.22, 0.18) if shards else 1.0
    drawn = jax.random.normal(stream_key, dims, jnp.float32) * deviation * gain
    return jnp.minimum(jnp.maximum(drawn, -reach), reach).astype(held_as)


def setup_inputs(seed: int = 0) -> dict:
    streams_of = jax.random.split(jax.random.key(seed), 5)
    return {
        "hidden": bell_draw(streams_of[0], (REPLICAS, TOKENS, FF), 1.0, 6.0, ((0, 8), (1, 32))),
        "out_grad": bell_draw(streams_of[1], (REPLICAS, TOKENS, D), 1.0, 6.0, ((0, 8), (1, 32))),
        "weights": bell_draw(streams_of[2], (REPLICAS, FF, D), 1.0, 6.0, ((0, 8), (1, 32)), jnp.float32),
        "round_index": jax.random.randint(streams_of[3], (1,), 0, 8).astype(jnp.int32),
    }


def reference(hidden, out_grad, weights, round_index):
    scale = FF ** -0.5

    def one_replica(items):
        acts, cotangent, master = items
        grad = jnp.dot(acts.T, cotangent, preferred_element_type=jnp.float32) * scale
        compute = master.astype(jnp.bfloat16)
        back = (jnp.dot(cotangent, compute.T, preferred_element_type=jnp.float32) * scale).astype(jnp.bfloat16)
        return grad, back

    grads, hidden_grad = lax.map(one_replica, (hidden, out_grad, weights))
    rate = 4.0 / (8.0 + round_index[0].astype(jnp.float32))
    stepped = weights - rate * grads
    levels = N_REPLICA.bit_length() - 1
    state = stepped
    for turn in range(2):
        exponent = ((round_index[0] + turn) % levels).astype(jnp.int32)
        offset = jnp.left_shift(jnp.ones((), jnp.int32), exponent)
        state = 0.5 * (state + jnp.roll(state, offset, axis=0))
    return state, hidden_grad
```

```python
from functools import partial

import jax
import jax.numpy as jnp
from jax import lax
from jax.experimental import pallas as pl
from jax.experimental.pallas import tpu as pltpu
from jax.sharding import PartitionSpec as P

FF = 11008
SCALE = FF ** (-0.5)
LANES = 128
HOME = 344
PAIR = 2 * HOME
VMEM = pl.BlockSpec(memory_space=pltpu.VMEM)
SMEM = pl.BlockSpec(memory_space=pltpu.SMEM)
PARAMS = pltpu.CompilerParams(vmem_limit_bytes=56 * 1024 * 1024)

CORE, Z0, Z1 = 1, 2, 4


def swap(value, mask):
    count = lax.axis_size("shard")
    return lax.ppermute(value, "shard", [(s, s ^ mask) for s in range(count)])


def forward(value, steps):
    count = lax.axis_size("replica")
    return lax.ppermute(value, "replica", [(s, (s + steps) % count) for s in range(count)])


PLANE = [
    [x * 8 + z1 * 4 + z0 * 2 + c for x in range(4) for z0 in range(2)]
    for z1 in range(2)
    for c in range(2)
]
ROW = [[x * 8 + rest for x in range(4)] for rest in range(8)]


def exchange(value, groups):
    return lax.all_to_all(value, "shard", 0, 0, axis_index_groups=groups, tiled=True)


def pieces():
    for tile in range(FF // LANES):
        parts = []
        low = tile * LANES
        while low < (tile + 1) * LANES:
            pair = low // PAIR
            high = min((pair + 1) * PAIR, (tile + 1) * LANES)
            x, z1, z0 = pair // 4, pair // 2 % 2, pair % 2
            parts.append((low - tile * LANES, x * 2 + z0, z1, low - pair * PAIR, high - low))
            low = high
        yield tile, parts


def pack_kernel(hidden, out):
    for tile, parts in pieces():
        turned = hidden[:, tile * LANES : (tile + 1) * LANES].T
        for place, member, z1, row, rows in parts:
            out[member, z1, row : row + rows, :] = turned[place : place + rows]


def unpack_kernel(blocks, out):
    for tile, parts in pieces():
        rows = [blocks[member, z1, row : row + n, :] for _, member, z1, row, n in parts]
        whole = rows[0] if len(rows) == 1 else jnp.concatenate(rows, axis=0)
        out[:, tile * LANES : (tile + 1) * LANES] = whole.T


def pack(hidden):
    return pl.pallas_call(
        pack_kernel,
        out_shape=jax.ShapeDtypeStruct((8, 2, PAIR, LANES), jnp.bfloat16),
        in_specs=[VMEM],
        out_specs=VMEM,
        compiler_params=PARAMS,
    )(hidden)


def unpack(blocks):
    return pl.pallas_call(
        unpack_kernel,
        out_shape=jax.ShapeDtypeStruct((LANES, FF), jnp.bfloat16),
        in_specs=[VMEM],
        out_specs=VMEM,
        compiler_params=PARAMS,
    )(blocks)


def grad_kernel(place, hidden, rows, mine, peer, left):
    core, z0, z1 = place[0], place[1], place[2]
    for x in range(4):
        for r in range(2):
            for z in range(2):
                left[z * PAIR : (z + 1) * PAIR, (x * 2 + r) * LANES : (x * 2 + r + 1) * LANES] = hidden[
                    x * 2 + (z0 ^ r), z
                ]
    width = rows.shape[-1]
    step = 256
    for n in range(0, width, step):
        right = rows[:, :, :, n : n + step].reshape(8 * LANES, step)
        for z in range(2):
            total = jnp.dot(
                left[z * PAIR : (z + 1) * PAIR, :], right, preferred_element_type=jnp.float32
            )
            first, second = total[:HOME], total[HOME:]
            mine[z ^ z1, :, n : n + step] = jnp.where(core == 0, first, second)
            peer[z ^ z1, :, n : n + step] = jnp.where(core == 0, second, first).astype(jnp.bfloat16)


def grad_part(place, hidden, rows):
    width = rows.shape[-1]
    return pl.pallas_call(
        grad_kernel,
        out_shape=(
            jax.ShapeDtypeStruct((2, HOME, width), jnp.float32),
            jax.ShapeDtypeStruct((2, HOME, width), jnp.bfloat16),
        ),
        in_specs=[SMEM, VMEM, VMEM],
        out_specs=(VMEM, VMEM),
        scratch_shapes=[pltpu.VMEM((2 * PAIR, 8 * LANES), jnp.bfloat16)],
        compiler_params=PARAMS,
    )(place, hidden, rows)


def back_kernel(place, rows_a, rows_b, own, across, over, over_across, out):
    core, z0, z1 = place[0], place[1], place[2]
    half = rows_a.shape[-1]
    for x in range(4):
        first = rows_a[x].reshape(2 * LANES, half)
        second = rows_b[x].reshape(2 * LANES, half)

        def product(weights):
            dims = (((1,), (1,)), ((), ()))
            total = lax.dot_general(
                weights[:, :half], first, dims, preferred_element_type=jnp.float32
            ) + lax.dot_general(
                weights[:, half:], second, dims, preferred_element_type=jnp.float32
            )
            return total * SCALE

        for z, (here, there) in enumerate(((own, across), (over, over_across))):
            a, b = product(here), product(there)
            whole = jnp.concatenate(
                [jnp.where(core == 0, a, b), jnp.where(core == 0, b, a)], axis=0
            ).astype(jnp.bfloat16)
            for r in range(2):
                out[x * 2 + (z0 ^ r), z ^ z1] = whole[:, r * LANES : (r + 1) * LANES]


def back_part(place, rows_a, rows_b, own, across, over, over_across):
    return pl.pallas_call(
        back_kernel,
        out_shape=jax.ShapeDtypeStruct((8, 2, PAIR, LANES), jnp.bfloat16),
        in_specs=[SMEM] + [VMEM] * 6,
        out_specs=VMEM,
        compiler_params=PARAMS,
    )(place, rows_a, rows_b, own, across, over, over_across)


def on_device(hidden, out_grad, weights, round_index):
    levels = lax.axis_size("replica").bit_length() - 1
    rate = 4.0 / (8.0 + round_index[0].astype(jnp.float32))
    pull = rate * SCALE
    shard = lax.axis_index("shard")
    place = jnp.stack([shard & 1, (shard >> 1) & 1, (shard >> 2) & 1]).astype(jnp.int32)

    master = weights[0]
    cotangent = out_grad[0]
    half = cotangent.shape[1] // 2
    beside = jnp.stack([cotangent, swap(cotangent, Z0)])
    units = exchange(pack(hidden[0]), PLANE)
    rows = [
        exchange(jnp.broadcast_to(part[None], (4,) + part.shape), ROW)
        for part in (beside[:, :, :half], beside[:, :, half:])
    ]
    own = master.astype(jnp.bfloat16)
    across = swap(own, CORE)
    over = swap(own, Z1)
    over_across = swap(over, CORE)

    def rest(units, rows_a, rows_b, own, across, over, over_across, master, steps):
        done = []
        for part, given in enumerate((rows_a, rows_b)):
            mine, peer = grad_part(place, units, given)
            met = mine + swap(peer, CORE).astype(jnp.float32)
            total = met[0] + swap(met[1].astype(jnp.bfloat16), Z1).astype(jnp.float32)
            state = master[:, part * half : (part + 1) * half] - pull * total
            for step in steps:
                state = 0.5 * (state + forward(state.astype(jnp.bfloat16), step).astype(jnp.float32))
            done.append(state)
        turned = back_part(place, rows_a, rows_b, own, across, over, over_across)
        hidden_grad = unpack(exchange(turned, PLANE))
        return jnp.concatenate(done, axis=1)[None], hidden_grad[None]

    branches = []
    for level in range(levels):
        steps = sorted((2**level, 2 ** ((level + 1) % levels)), reverse=True)
        branches.append(partial(rest, steps=steps))
    return lax.switch(
        round_index[0] % levels,
        branches,
        units,
        rows[0],
        rows[1],
        own,
        across,
        over,
        over_across,
        master,
    )


def solution(mesh):
    placed = P("replica", "shard", None)
    return jax.shard_map(
        on_device,
        mesh=mesh,
        in_specs=(placed, placed, placed, P()),
        out_specs=(placed, placed),
        check_vma=False,
    )
```

```python
from functools import partial

import jax
import jax.numpy as jnp
from jax import lax
from jax.experimental import pallas as pl
from jax.experimental.pallas import tpu as pltpu
from jax.sharding import PartitionSpec as P

FF = 11008
SCALE = FF ** (-0.5)
LANES = 128
HOME = 344
PAIR = 2 * HOME
STEP = 512
EARLY = 512
VMEM = pl.BlockSpec(memory_space=pltpu.VMEM)
SMEM = pl.BlockSpec(memory_space=pltpu.SMEM)
PARAMS = pltpu.CompilerParams(vmem_limit_bytes=56 * 1024 * 1024)

CORE, Z0, Z1 = 1, 2, 4


def swap(value, mask):
    count = lax.axis_size("shard")
    return lax.ppermute(value, "shard", [(s, s ^ mask) for s in range(count)])


def along_x(value, steps):
    count = lax.axis_size("shard")
    return lax.ppermute(value, "shard", [(s, (s + 8 * steps) % count) for s in range(count)])


def after(value, *others):
    return lax.optimization_barrier((value, others))[0]


def cost(flops, moved):
    return pl.CostEstimate(flops=flops, bytes_accessed=moved, transcendentals=0)


def forward(value, steps):
    count = lax.axis_size("replica")
    return lax.ppermute(value, "replica", [(s, (s + steps) % count) for s in range(count)])


PLANE = [
    [x * 8 + z1 * 4 + z0 * 2 + c for x in range(4) for z0 in range(2)]
    for z1 in range(2)
    for c in range(2)
]


def exchange(value, groups):
    return lax.all_to_all(value, "shard", 0, 0, axis_index_groups=groups, tiled=True)


def pieces():
    for tile in range(FF // LANES):
        parts = []
        low = tile * LANES
        while low < (tile + 1) * LANES:
            pair = low // PAIR
            high = min((pair + 1) * PAIR, (tile + 1) * LANES)
            x, z1, z0 = pair // 4, pair // 2 % 2, pair % 2
            parts.append((low - tile * LANES, x * 2 + z0, z1, low - pair * PAIR, high - low))
            low = high
        yield tile, parts


def pack_kernel(hidden, out):
    for tile, parts in pieces():
        turned = hidden[:, tile * LANES : (tile + 1) * LANES].T
        for place, member, z1, row, rows in parts:
            out[member, z1, row : row + rows, :] = turned[place : place + rows]


def unpack_kernel(blocks, out):
    for tile, parts in pieces():
        rows = [blocks[member, z1, row : row + n, :] for _, member, z1, row, n in parts]
        whole = rows[0] if len(rows) == 1 else jnp.concatenate(rows, axis=0)
        out[:, tile * LANES : (tile + 1) * LANES] = whole.T


def pack(hidden):
    return pl.pallas_call(
        pack_kernel,
        out_shape=jax.ShapeDtypeStruct((8, 2, PAIR, LANES), jnp.bfloat16),
        in_specs=[VMEM],
        out_specs=VMEM,
        compiler_params=PARAMS,
        cost_estimate=cost(0, 0),
    )(hidden)


def unpack(blocks):
    return pl.pallas_call(
        unpack_kernel,
        out_shape=jax.ShapeDtypeStruct((LANES, FF), jnp.bfloat16),
        in_specs=[VMEM],
        out_specs=VMEM,
        compiler_params=PARAMS,
        cost_estimate=cost(0, 0),
    )(blocks)


def source(place, steps, r):
    return ((place[3] - steps) & 3) * 2 + (place[1] ^ r)


def grad_kernel(place, hidden, *refs):
    (near, far, near1, far1, near3, far3, two), (mine, peer, left) = refs[:7], refs[7:]
    core, z1 = place[0], place[2]

    @pl.when(pl.program_id(0) == 0)
    def _():
        for index in range(8):
            member = source(place, index // 2, index % 2)
            for z in range(2):
                left[z * PAIR : (z + 1) * PAIR, index * LANES : (index + 1) * LANES] = hidden[
                    member, z
                ]

    rows = [near[...], far[...], near1[...], far1[...], two[0], two[1], near3[...], far3[...]]
    right = jnp.concatenate(rows, axis=0)
    for z in range(2):
        total = jnp.dot(
            left[z * PAIR : (z + 1) * PAIR, :], right, preferred_element_type=jnp.float32
        )
        first, second = total[:HOME], total[HOME:]
        mine[z ^ z1] = jnp.where(core == 0, first, second).astype(jnp.bfloat16)
        peer[z ^ z1] = jnp.where(core == 0, second, first).astype(jnp.bfloat16)


def grad_part(place, hidden, rows, two, part):
    width = two.shape[2]
    at = part * width // STEP
    columns = pl.BlockSpec((LANES, STEP), lambda n: (0, at + n))
    given = pl.BlockSpec((2, LANES, STEP), lambda n: (0, 0, n))
    both = pl.BlockSpec((2, HOME, STEP), lambda n: (0, 0, n))
    return pl.pallas_call(
        grad_kernel,
        grid=(width // STEP,),
        out_shape=(jax.ShapeDtypeStruct((2, HOME, width), jnp.bfloat16),) * 2,
        in_specs=[SMEM, VMEM] + [columns] * 6 + [given],
        out_specs=(both, both),
        scratch_shapes=[pltpu.VMEM((2 * PAIR, 8 * LANES), jnp.bfloat16)],
        compiler_params=PARAMS,
        cost_estimate=cost(0, 0),
    )(place, hidden, *rows, two)


def back_kernel(place, near, far, near1, far1, near3, far3, two_a, two_b, own, paired, out):
    core, z1 = place[0], place[2]
    for steps, group in ((0, (near, far)), (1, (near1, far1)), (2, None), (3, (near3, far3))):
        if group is None:
            right = jnp.concatenate(
                [two.reshape(2 * LANES, two.shape[2]) for two in (two_a[...], two_b[...])], axis=1
            )
        else:
            right = jnp.concatenate([group[0][...], group[1][...]], axis=0)

        def product(weights, z):
            dims = (((1,), (1,)), ((), ()))
            return SCALE * lax.dot_general(
                weights[z], right, dims, preferred_element_type=jnp.float32
            )

        for z in range(2):
            a, b = product(own, z), product(paired, z)
            whole = jnp.concatenate(
                [jnp.where(core == 0, a, b), jnp.where(core == 0, b, a)], axis=0
            ).astype(jnp.bfloat16)
            for r in range(2):
                out[source(place, steps, r), z ^ z1] = whole[:, r * LANES : (r + 1) * LANES]


def back_part(place, rows, two_a, two_b, own, paired):
    return pl.pallas_call(
        back_kernel,
        out_shape=jax.ShapeDtypeStruct((8, 2, PAIR, LANES), jnp.bfloat16),
        in_specs=[SMEM] + [VMEM] * 10,
        out_specs=VMEM,
        compiler_params=PARAMS,
        cost_estimate=cost(0, 0),
    )(place, *rows, two_a, two_b, own, paired)


def widen(value):
    return value.astype(jnp.float32)


def narrow(value):
    return value.astype(jnp.bfloat16)


def meet(mine, peer):
    return widen(mine[0]) + widen(peer[0]), narrow(widen(mine[1]) + widen(peer[1]))


def mix(state, steps):
    return 0.5 * (state + widen(forward(narrow(state), steps)))


def gossip_early(keep, other, master, pull, steps):
    state = mix(master[:, : keep.shape[1]] - pull * (keep + widen(other)), steps[0])
    return state if 1 in steps else mix(state, steps[1])


def gossip_late(early, keep, other, master, pull, steps):
    state = mix(master[:, early.shape[1] :] - pull * (keep + widen(other)), steps[0])
    if 1 in steps:
        early = mix(early, steps[1])
    return jnp.concatenate([early, mix(state, steps[1])], axis=1)


def on_device(hidden, out_grad, weights, round_index):
    levels = lax.axis_size("replica").bit_length() - 1
    pull = SCALE * 4.0 / (8.0 + round_index[0].astype(jnp.float32))
    shard = lax.axis_index("shard")
    place = jnp.stack([shard & 1, (shard >> 1) & 1, (shard >> 2) & 1, shard >> 3]).astype(jnp.int32)

    master = weights[0]
    near = out_grad[0]
    half = near.shape[1] // 2
    far = swap(near, Z0)
    near1, near3 = along_x(near, 1), along_x(near, 3)
    over_first = swap(narrow(master[:, :EARLY]), Z1)
    packed, far_later, master_later = after(
        (pack(hidden[0]), far, master), near1, near3, over_first
    )
    units = exchange(packed, PLANE)
    far1, far3 = along_x(far_later, 1), along_x(far_later, 3)
    over_last = swap(narrow(master_later[:, EARLY:]), Z1)
    two_a = along_x(jnp.stack([near1[:, :half], far1[:, :half]]), 1)
    two_b = along_x(jnp.stack([near3[:, half:], far3[:, half:]]), 3)
    units, over_last, two_a, two_b = lax.optimization_barrier((units, over_last, two_a, two_b))
    rows = [near, far, near1, far1, near3, far3]

    mine_a, peer_a = grad_part(place, units, rows, two_a, 0)
    keep_a, send_a = meet(mine_a, swap(peer_a, CORE))
    from_a = swap(send_a, Z1)
    both = jnp.stack([narrow(master), jnp.concatenate([over_first, over_last], axis=1)])
    paired = swap(after(both, send_a), CORE)
    mine_b, peer_b = grad_part(place, after(units, send_a), rows, two_b, 1)
    turned = back_part(place, rows, two_a, two_b, both, after(paired, peer_b))
    peer_b, turned = after((peer_b, turned), from_a)
    back = exchange(turned, PLANE)
    keep_b, send_b = meet(mine_b, swap(peer_b, CORE))
    from_b = swap(send_b, Z1)

    level = round_index[0] % levels
    pairs = [
        sorted((2**first, 2 ** ((first + 1) % levels)), reverse=True) for first in range(levels)
    ]
    early = lax.switch(
        level,
        [partial(gossip_early, steps=steps) for steps in pairs],
        keep_a,
        after(from_a, send_b),
        master,
        pull,
    )
    from_b, early = lax.optimization_barrier((from_b, early))
    averaged = lax.switch(
        level,
        [partial(gossip_late, steps=steps) for steps in pairs],
        early,
        keep_b,
        from_b,
        master,
        pull,
    )
    return averaged[None], unpack(back)[None]


def solution(mesh):
    placed = P("replica", "shard", None)
    return jax.shard_map(
        on_device,
        mesh=mesh,
        in_specs=(placed, placed, placed, P()),
        out_specs=(placed, placed),
        check_vma=False,
    )
```

```python
from functools import partial

import jax
import jax.numpy as jnp
from jax import lax
from jax.experimental import pallas as pl
from jax.experimental.pallas import tpu as pltpu
from jax.sharding import PartitionSpec as P

FF = 11008
SCALE = FF ** (-0.5)
LANES = 128
HOME = 344
PAIR = 2 * HOME
STEP = 512
EARLY = 512
VMEM = pl.BlockSpec(memory_space=pltpu.VMEM)
SMEM = pl.BlockSpec(memory_space=pltpu.SMEM)
PARAMS = pltpu.CompilerParams(vmem_limit_bytes=56 * 1024 * 1024)

CORE, Z0, Z1 = 1, 2, 4


def swap(value, mask):
    count = lax.axis_size("shard")
    return lax.ppermute(value, "shard", [(s, s ^ mask) for s in range(count)])


def along_x(value, steps):
    count = lax.axis_size("shard")
    return lax.ppermute(value, "shard", [(s, (s + 8 * steps) % count) for s in range(count)])


def after(value, *others):
    return lax.optimization_barrier((value, others))[0]


def cost(flops, moved):
    return pl.CostEstimate(flops=flops, bytes_accessed=moved, transcendentals=0)


def forward(value, steps):
    count = lax.axis_size("replica")
    return lax.ppermute(value, "replica", [(s, (s + steps) % count) for s in range(count)])


PLANE = [
    [x * 8 + z1 * 4 + z0 * 2 + c for x in range(4) for z0 in range(2)]
    for z1 in range(2)
    for c in range(2)
]


def exchange(value, groups):
    return lax.all_to_all(value, "shard", 0, 0, axis_index_groups=groups, tiled=True)


def pieces():
    for tile in range(FF // LANES // 2):
        parts = []
        low = tile * LANES
        while low < (tile + 1) * LANES:
            pair = low // PAIR
            high = min((pair + 1) * PAIR, (tile + 1) * LANES)
            x, z1, z0 = pair // 4, pair // 2 % 2, pair % 2
            parts.append((low - tile * LANES, x * 2 + z0, z1, low - pair * PAIR, high - low))
            low = high
        yield tile, parts


def pack_kernel(hidden, out):
    for tile, parts in pieces():
        turned = hidden[:, tile * LANES : (tile + 1) * LANES].T
        for place, member, z1, row, rows in parts:
            out[member, z1, row : row + rows, :] = turned[place : place + rows]


def unpack_kernel(blocks, out):
    for tile, parts in pieces():
        rows = [blocks[member, z1, row : row + n, :] for _, member, z1, row, n in parts]
        whole = rows[0] if len(rows) == 1 else jnp.concatenate(rows, axis=0)
        out[:, tile * LANES : (tile + 1) * LANES] = whole.T


HALF_WIDE = pl.BlockSpec((LANES, FF // 2), lambda n: (0, n))
HALF_BLOCKS = pl.BlockSpec((4, 2, PAIR, LANES), lambda n: (n, 0, 0, 0))


def pack(hidden):
    return pl.pallas_call(
        pack_kernel,
        grid=(2,),
        out_shape=jax.ShapeDtypeStruct((8, 2, PAIR, LANES), jnp.bfloat16),
        in_specs=[HALF_WIDE],
        out_specs=HALF_BLOCKS,
        compiler_params=PARAMS,
        cost_estimate=cost(0, 0),
    )(hidden)


def unpack(blocks):
    return pl.pallas_call(
        unpack_kernel,
        grid=(2,),
        out_shape=jax.ShapeDtypeStruct((LANES, FF), jnp.bfloat16),
        in_specs=[HALF_BLOCKS],
        out_specs=HALF_WIDE,
        compiler_params=PARAMS,
        cost_estimate=cost(0, 0),
    )(blocks)


def source(place, steps, r):
    return ((place[3] - steps) & 3) * 2 + (place[1] ^ r)


def grad_kernel(place, hidden, *refs):
    (near, far, near1, far1, near3, far3, two), (mine, peer, left) = refs[:7], refs[7:]
    core, z1 = place[0], place[2]

    @pl.when(pl.program_id(0) == 0)
    def _():
        for index in range(8):
            member = source(place, index // 2, index % 2)
            for z in range(2):
                left[z * PAIR : (z + 1) * PAIR, index * LANES : (index + 1) * LANES] = hidden[
                    member, z
                ]

    rows = [near[...], far[...], near1[...], far1[...], two[0], two[1], near3[...], far3[...]]
    right = jnp.concatenate(rows, axis=0)
    for z in range(2):
        total = jnp.dot(
            left[z * PAIR : (z + 1) * PAIR, :], right, preferred_element_type=jnp.float32
        )
        first, second = total[:HOME], total[HOME:]
        mine[z ^ z1] = jnp.where(core == 0, first, second).astype(jnp.bfloat16)
        peer[z ^ z1] = jnp.where(core == 0, second, first).astype(jnp.bfloat16)


def grad_part(place, hidden, rows, two, part):
    width = two.shape[2]
    at = part * width // STEP
    columns = pl.BlockSpec((LANES, STEP), lambda n: (0, at + n))
    given = pl.BlockSpec((2, LANES, STEP), lambda n: (0, 0, n))
    both = pl.BlockSpec((2, HOME, STEP), lambda n: (0, 0, n))
    return pl.pallas_call(
        grad_kernel,
        grid=(width // STEP,),
        out_shape=(jax.ShapeDtypeStruct((2, HOME, width), jnp.bfloat16),) * 2,
        in_specs=[SMEM, VMEM] + [columns] * 6 + [given],
        out_specs=(both, both),
        scratch_shapes=[pltpu.VMEM((2 * PAIR, 8 * LANES), jnp.bfloat16)],
        compiler_params=PARAMS,
        cost_estimate=cost(0, 0),
    )(place, hidden, *rows, two)


def back_kernel(place, near, far, near1, far1, near3, far3, two_a, two_b, own, paired, out):
    core, z1 = place[0], place[2]
    for steps, group in ((0, (near, far)), (1, (near1, far1)), (2, None), (3, (near3, far3))):
        if group is None:
            right = jnp.concatenate(
                [two.reshape(2 * LANES, two.shape[2]) for two in (two_a[...], two_b[...])], axis=1
            )
        else:
            right = jnp.concatenate([group[0][...], group[1][...]], axis=0)

        def product(weights, z):
            dims = (((1,), (1,)), ((), ()))
            return SCALE * lax.dot_general(
                weights[z], right, dims, preferred_element_type=jnp.float32
            )

        for z in range(2):
            a, b = product(own, z), product(paired, z)
            whole = jnp.concatenate(
                [jnp.where(core == 0, a, b), jnp.where(core == 0, b, a)], axis=0
            ).astype(jnp.bfloat16)
            for r in range(2):
                out[source(place, steps, r), z ^ z1] = whole[:, r * LANES : (r + 1) * LANES]


def back_part(place, rows, two_a, two_b, own, paired):
    return pl.pallas_call(
        back_kernel,
        out_shape=jax.ShapeDtypeStruct((8, 2, PAIR, LANES), jnp.bfloat16),
        in_specs=[SMEM] + [VMEM] * 10,
        out_specs=VMEM,
        compiler_params=PARAMS,
        cost_estimate=cost(0, 0),
    )(place, *rows, two_a, two_b, own, paired)


def widen(value):
    return value.astype(jnp.float32)


def narrow(value):
    return value.astype(jnp.bfloat16)


def meet(mine, peer):
    return widen(mine[0]) + widen(peer[0]), narrow(widen(mine[1]) + widen(peer[1]))


def mix(state, steps):
    return 0.5 * (state + widen(forward(narrow(state), steps)))


def mix_both_ways(state, steps):
    half = state.shape[1] // 2
    return jnp.concatenate([mix(state[:, :half], steps), mix(state[:, half:], -steps)], axis=1)


def second_round(state, steps):
    count = lax.axis_size("replica")
    if 2 * steps[0] == count and 4 * steps[1] == count:
        return mix_both_ways(state, steps[1])
    return mix(state, steps[1])


def gossip_early(keep, other, master, pull, steps):
    state = mix(master[:, : keep.shape[1]] - pull * (keep + widen(other)), steps[0])
    return state if 1 in steps else second_round(state, steps)


def gossip_late(early, keep, other, master, pull, steps):
    state = mix(master[:, early.shape[1] :] - pull * (keep + widen(other)), steps[0])
    if 1 in steps:
        early = mix(early, steps[1])
    return jnp.concatenate([early, second_round(state, steps)], axis=1)


def on_device(hidden, out_grad, weights, round_index):
    levels = lax.axis_size("replica").bit_length() - 1
    pull = SCALE * 4.0 / (8.0 + round_index[0].astype(jnp.float32))
    shard = lax.axis_index("shard")
    place = jnp.stack([shard & 1, (shard >> 1) & 1, (shard >> 2) & 1, shard >> 3]).astype(jnp.int32)

    master = weights[0]
    near = out_grad[0]
    half = near.shape[1] // 2
    far = swap(near, Z0)
    near1, near3 = along_x(near, 1), along_x(near, 3)
    over_first = swap(narrow(master[:, :EARLY]), Z1)
    packed, far_later, master_later = after(
        (pack(hidden[0]), far, master), near1, near3, over_first
    )
    units = exchange(packed, PLANE)
    far1, far3 = along_x(far_later, 1), along_x(far_later, 3)
    over_last = swap(narrow(master_later[:, EARLY:]), Z1)
    two_a = along_x(jnp.stack([near1[:, :half], far1[:, :half]]), 1)
    two_b = along_x(jnp.stack([near3[:, half:], far3[:, half:]]), 3)
    units, over_last, two_a, two_b = lax.optimization_barrier((units, over_last, two_a, two_b))
    rows = [near, far, near1, far1, near3, far3]

    mine_a, peer_a = grad_part(place, units, rows, two_a, 0)
    keep_a, send_a = meet(mine_a, swap(peer_a, CORE))
    from_a = swap(send_a, Z1)
    both = jnp.stack([narrow(master), jnp.concatenate([over_first, over_last], axis=1)])
    paired = swap(after(both, send_a), CORE)
    mine_b, peer_b = grad_part(place, after(units, send_a), rows, two_b, 1)
    turned = back_part(place, rows, two_a, two_b, both, after(paired, peer_b))
    peer_b, turned = after((peer_b, turned), from_a)
    back = exchange(turned, PLANE)
    keep_b, send_b = meet(mine_b, swap(peer_b, CORE))
    from_b = swap(send_b, Z1)

    level = round_index[0] % levels
    pairs = [
        sorted((2**first, 2 ** ((first + 1) % levels)), reverse=True) for first in range(levels)
    ]
    early = lax.switch(
        level,
        [partial(gossip_early, steps=steps) for steps in pairs],
        keep_a,
        after(from_a, send_b),
        master,
        pull,
    )
    from_b, early = lax.optimization_barrier((from_b, early))
    averaged = lax.switch(
        level,
        [partial(gossip_late, steps=steps) for steps in pairs],
        early,
        keep_b,
        from_b,
        master,
        pull,
    )
    return averaged[None], unpack(back)[None]


def solution(mesh):
    placed = P("replica", "shard", None)
    return jax.shard_map(
        on_device,
        mesh=mesh,
        in_specs=(placed, placed, placed, P()),
        out_specs=(placed, placed),
        check_vma=False,
    )
```

```python
from functools import partial

import jax
import jax.numpy as jnp
from jax import lax
from jax.experimental import pallas as pl
from jax.experimental.pallas import tpu as pltpu
from jax.sharding import PartitionSpec as P

FF = 11008
SCALE = FF ** (-0.5)
LANES = 128
HOME = 344
PAIR = 2 * HOME
STEP = 512
EARLY = 512
VMEM = pl.BlockSpec(memory_space=pltpu.VMEM)
SMEM = pl.BlockSpec(memory_space=pltpu.SMEM)
PARAMS = pltpu.CompilerParams(vmem_limit_bytes=56 * 1024 * 1024)

CORE, Z0, Z1 = 1, 2, 4


def swap(value, mask):
    count = lax.axis_size("shard")
    return lax.ppermute(value, "shard", [(s, s ^ mask) for s in range(count)])


def along_x(value, steps):
    count = lax.axis_size("shard")
    return lax.ppermute(value, "shard", [(s, (s + 8 * steps) % count) for s in range(count)])


def after(value, *others):
    return lax.optimization_barrier((value, others))[0]


def cost(flops, moved):
    return pl.CostEstimate(flops=flops, bytes_accessed=moved, transcendentals=0)


def forward(value, steps):
    count = lax.axis_size("replica")
    return lax.ppermute(value, "replica", [(s, (s + steps) % count) for s in range(count)])


PLANE = [
    [x * 8 + z1 * 4 + z0 * 2 + c for x in range(4) for z0 in range(2)]
    for z1 in range(2)
    for c in range(2)
]


def exchange(value, groups):
    return lax.all_to_all(value, "shard", 0, 0, axis_index_groups=groups, tiled=True)


def pieces():
    for tile in range(FF // LANES // 2):
        parts = []
        low = tile * LANES
        while low < (tile + 1) * LANES:
            pair = low // PAIR
            high = min((pair + 1) * PAIR, (tile + 1) * LANES)
            x, z1, z0 = pair // 4, pair // 2 % 2, pair % 2
            parts.append((low - tile * LANES, x * 2 + z0, z1, low - pair * PAIR, high - low))
            low = high
        yield tile, parts


def pack_kernel(hidden, out):
    for tile, parts in pieces():
        turned = hidden[:, tile * LANES : (tile + 1) * LANES].T
        for place, member, z1, row, rows in parts:
            out[member, z1, row : row + rows, :] = turned[place : place + rows]


def unpack_kernel(blocks, out):
    for tile, parts in pieces():
        rows = [blocks[member, z1, row : row + n, :] for _, member, z1, row, n in parts]
        whole = rows[0] if len(rows) == 1 else jnp.concatenate(rows, axis=0)
        out[:, tile * LANES : (tile + 1) * LANES] = whole.T


HALF_WIDE = pl.BlockSpec((LANES, FF // 2), lambda n: (0, n))
HALF_BLOCKS = pl.BlockSpec((4, 2, PAIR, LANES), lambda n: (n, 0, 0, 0))


def pack(hidden):
    return pl.pallas_call(
        pack_kernel,
        grid=(2,),
        out_shape=jax.ShapeDtypeStruct((8, 2, PAIR, LANES), jnp.bfloat16),
        in_specs=[HALF_WIDE],
        out_specs=HALF_BLOCKS,
        compiler_params=PARAMS,
        cost_estimate=cost(0, 0),
    )(hidden)


def unpack(blocks):
    return pl.pallas_call(
        unpack_kernel,
        grid=(2,),
        out_shape=jax.ShapeDtypeStruct((LANES, FF), jnp.bfloat16),
        in_specs=[HALF_BLOCKS],
        out_specs=HALF_WIDE,
        compiler_params=PARAMS,
        cost_estimate=cost(0, 0),
    )(blocks)


def source(place, steps, r):
    return ((place[3] - steps) & 3) * 2 + (place[1] ^ r)


def grad_kernel(place, hidden, *refs):
    (near, far, near1, far1, near3, far3, two), (mine, peer, left) = refs[:7], refs[7:]
    core, z1 = place[0], place[2]

    @pl.when(pl.program_id(0) == 0)
    def _():
        for index in range(8):
            member = source(place, index // 2, index % 2)
            for z in range(2):
                left[z * PAIR : (z + 1) * PAIR, index * LANES : (index + 1) * LANES] = hidden[
                    member, z
                ]

    rows = [near[...], far[...], near1[...], far1[...], two[0], two[1], near3[...], far3[...]]
    right = jnp.concatenate(rows, axis=0)
    for z in range(2):
        total = jnp.dot(
            left[z * PAIR : (z + 1) * PAIR, :], right, preferred_element_type=jnp.float32
        )
        first, second = total[:HOME], total[HOME:]
        mine[z ^ z1] = jnp.where(core == 0, first, second).astype(jnp.bfloat16)
        peer[z ^ z1] = jnp.where(core == 0, second, first).astype(jnp.bfloat16)


def grad_part(place, hidden, rows, two, part):
    width = two.shape[2]
    at = part * width // STEP
    columns = pl.BlockSpec((LANES, STEP), lambda n: (0, at + n))
    given = pl.BlockSpec((2, LANES, STEP), lambda n: (0, 0, n))
    both = pl.BlockSpec((2, HOME, STEP), lambda n: (0, 0, n))
    return pl.pallas_call(
        grad_kernel,
        grid=(width // STEP,),
        out_shape=(jax.ShapeDtypeStruct((2, HOME, width), jnp.bfloat16),) * 2,
        in_specs=[SMEM, VMEM] + [columns] * 6 + [given],
        out_specs=(both, both),
        scratch_shapes=[pltpu.VMEM((2 * PAIR, 8 * LANES), jnp.bfloat16)],
        compiler_params=PARAMS,
        cost_estimate=cost(0, 0),
    )(place, hidden, *rows, two)


def back_kernel(place, near, far, near1, far1, near3, far3, two_a, two_b, own, paired, out):
    core, z1 = place[0], place[2]
    for steps, group in ((0, (near, far)), (1, (near1, far1)), (2, None), (3, (near3, far3))):
        if group is None:
            right = jnp.concatenate(
                [two.reshape(2 * LANES, two.shape[2]) for two in (two_a[...], two_b[...])], axis=1
            )
        else:
            right = jnp.concatenate([group[0][...], group[1][...]], axis=0)

        def product(weights, z):
            dims = (((1,), (1,)), ((), ()))
            return SCALE * lax.dot_general(
                weights[z], right, dims, preferred_element_type=jnp.float32
            )

        for z in range(2):
            a, b = product(own, z), product(paired, z)
            whole = jnp.concatenate(
                [jnp.where(core == 0, a, b), jnp.where(core == 0, b, a)], axis=0
            ).astype(jnp.bfloat16)
            for r in range(2):
                out[source(place, steps, r), z ^ z1] = whole[:, r * LANES : (r + 1) * LANES]


def back_part(place, rows, two_a, two_b, own, paired):
    return pl.pallas_call(
        back_kernel,
        out_shape=jax.ShapeDtypeStruct((8, 2, PAIR, LANES), jnp.bfloat16),
        in_specs=[SMEM] + [VMEM] * 10,
        out_specs=VMEM,
        compiler_params=PARAMS,
        cost_estimate=cost(0, 0),
    )(place, *rows, two_a, two_b, own, paired)


def widen(value):
    return value.astype(jnp.float32)


def narrow(value):
    return value.astype(jnp.bfloat16)


def meet(mine, peer):
    return widen(mine[0]) + widen(peer[0]), narrow(widen(mine[1]) + widen(peer[1]))


def mix(state, steps, *others):
    other = forward(narrow(state), steps)
    return 0.5 * (state + widen(after(other, *others) if others else other))


def mix_both_ways(state, steps, *others):
    half = state.shape[1] // 2
    ways = [mix(state[:, :half], steps, *others), mix(state[:, half:], -steps, *others)]
    return jnp.concatenate(ways, axis=1)


def second_round(state, steps, *others):
    count = lax.axis_size("replica")
    if 2 * steps[0] == count and 4 * steps[1] == count:
        return mix_both_ways(state, steps[1], *others)
    return mix(state, steps[1], *others)


def gossip_early(keep, other, master, pull, steps):
    state = mix(master[:, : keep.shape[1]] - pull * (keep + widen(other)), steps[0])
    return state if 1 in steps else second_round(state, steps)


def gossip_late(early, keep, other, master, pull, back, steps):
    hidden_grad = unpack(back)
    state = mix(master[:, early.shape[1] :] - pull * (keep + widen(other)), steps[0])
    if 1 in steps:
        early = mix(early, steps[1])
    averaged = jnp.concatenate([early, second_round(state, steps, hidden_grad)], axis=1)
    return averaged, hidden_grad


def on_device(hidden, out_grad, weights, round_index):
    levels = lax.axis_size("replica").bit_length() - 1
    pull = SCALE * 4.0 / (8.0 + round_index[0].astype(jnp.float32))
    shard = lax.axis_index("shard")
    place = jnp.stack([shard & 1, (shard >> 1) & 1, (shard >> 2) & 1, shard >> 3]).astype(jnp.int32)

    master = weights[0]
    near = out_grad[0]
    half = near.shape[1] // 2
    far = swap(near, Z0)
    near1, near3 = along_x(near, 1), along_x(near, 3)
    over_first = swap(narrow(master[:, :EARLY]), Z1)
    packed, far_later, master_later = after(
        (pack(hidden[0]), far, master), near1, near3, over_first
    )
    units = exchange(packed, PLANE)
    far1, far3 = along_x(far_later, 1), along_x(far_later, 3)
    over_last = swap(narrow(master_later[:, EARLY:]), Z1)
    two_a = along_x(jnp.stack([near1[:, :half], far1[:, :half]]), 1)
    two_b = along_x(jnp.stack([near3[:, half:], far3[:, half:]]), 3)
    units, over_last, two_a, two_b = lax.optimization_barrier((units, over_last, two_a, two_b))
    rows = [near, far, near1, far1, near3, far3]

    mine_a, peer_a = grad_part(place, units, rows, two_a, 0)
    keep_a, send_a = meet(mine_a, swap(peer_a, CORE))
    from_a = swap(send_a, Z1)
    both = jnp.stack([narrow(master), jnp.concatenate([over_first, over_last], axis=1)])
    paired = swap(after(both, send_a), CORE)
    mine_b, peer_b = grad_part(place, after(units, send_a), rows, two_b, 1)
    turned = back_part(place, rows, two_a, two_b, both, after(paired, peer_b))
    peer_b, turned = after((peer_b, turned), from_a)
    back = exchange(turned, PLANE)
    keep_b, send_b = meet(mine_b, swap(peer_b, CORE))
    from_b = swap(send_b, Z1)

    level = round_index[0] % levels
    pairs = [
        sorted((2**first, 2 ** ((first + 1) % levels)), reverse=True) for first in range(levels)
    ]
    early = lax.switch(
        level,
        [partial(gossip_early, steps=steps) for steps in pairs],
        keep_a,
        after(from_a, send_b),
        master,
        pull,
    )
    from_b, early = lax.optimization_barrier((from_b, early))
    averaged, hidden_grad = lax.switch(
        level,
        [partial(gossip_late, steps=steps) for steps in pairs],
        early,
        keep_b,
        from_b,
        master,
        pull,
        back,
    )
    return averaged[None], hidden_grad[None]


def solution(mesh):
    placed = P("replica", "shard", None)
    return jax.shard_map(
        on_device,
        mesh=mesh,
        in_specs=(placed, placed, placed, P()),
        out_specs=(placed, placed),
        check_vma=False,
    )
```
